512 devices in a mesh: group: 4 (over x), seq: 128 (over z, y, core).
Axes of the slice: x: 4, y: 8, z: 8, core: 2. Of those that a mesh axis runs over, the one named last changes fastest.
Arguments:
- query_vectors: bfloat16 [4, 3072, 4096], P('group', 'seq'), may hold values from -5 to 5
- key_vectors: bfloat16 [4, 3072, 4096], P('group', 'seq'), may hold values from -5 to 5
- value_vectors: bfloat16 [4, 3072, 4096], P('group', 'seq'), may hold values from -6 to 6
- levels: int32 [4], replicated, may hold values from 0 to 49
- causal_order: int32 [4], replicated, may hold values from 0 to 3999, as said below
- level_gates: float32 [50, 4096], replicated, may hold values from 0.25 to 2
Outputs:
- gated_attention: bfloat16 [4, 3072, 4096], P('group', 'seq')
The draws below stay inside these ranges and needn't reach their ends.
Inputs may be any that keep to these rules, and one draw needn't show every extreme that they name: `causal_order`: 4 distinct values.
All inputs are finite; a program needn't handle non-finite values.
Results may differ from the reference program's by a relative error of at most 0.013.
Values may be sent and summed in bfloat16 or wider, within the bound.
A program may use at most 64 MiB of HBM per device.

```python
import jax
import jax.numpy as jnp
from jax import lax

HEADS = 32
HD = 128
LEVELS = 50
D = 4096
GROUPS = 4
GROUP_LEN = 3072


def draw_query_vectors(key, part):
    key = jax.random.fold_in(key, 11)
    base = jnp.clip(jax.random.normal(key, (GROUPS, GROUP_LEN, HEADS * HD), jnp.float32), -5.0, 5.0)
    return base.astype(jnp.bfloat16)


def draw_key_vectors(key, part):
    key = jax.random.fold_in(key, 23)
    base = jnp.clip(jax.random.normal(key, (GROUPS, GROUP_LEN, HEADS * HD), jnp.float32), -5.0, 5.0)
    return base.astype(jnp.bfloat16)


def draw_causal_order(key, part):
    key = jax.random.fold_in(key, 37)
    rank_key, offset_key = jax.random.split(key)
    ranks = jax.random.permutation(rank_key, jnp.arange(GROUPS, dtype=jnp.int32))
    offsets = jax.random.randint(offset_key, (GROUPS,), 1, 999)
    offsets = jnp.where(ranks == 0, 0, jnp.where(ranks == GROUPS - 1, 999, offsets))
    return (ranks * 1000 + offsets).astype(jnp.int32)


def plant(values, rng, low, high):
    index_at = [jax.random.randint(jax.random.fold_in(rng, axis), (), 0, length) for axis, length in enumerate(values.shape)]
    longest = values.shape.index(max(values.shape))
    neighbour = index_at[:longest] + [(index_at[longest] + 1) % values.shape[longest]] + index_at[longest + 1:]
    return values.at[tuple(index_at)].set(low).at[tuple(neighbour)].set(high)


def steps_of(key, dims, cuts, low, largest):
    gain = 1.0
    for dim, parts in cuts:
        steps = jax.random.uniform(jax.random.fold_in(jax.random.fold_in(key, 6), dim), (parts,), jnp.float32, low / len(cuts), largest / len(cuts))
        gain = gain * jnp.repeat(jnp.exp(steps), dims[dim] // parts).reshape((-1,) + (1,) * (len(dims) - 1 - dim))
    return gain


def normal_values(key, extent, width, reach, shards=(), kind=jnp.bfloat16):
    gain = steps_of(key, extent, shards, -0.22, 0.18) if shards else 1.0
    result = jax.random.normal(key, extent, jnp.float32) * width * gain
    return jnp.minimum(jnp.maximum(result, -reach), reach).astype(kind)


def setup_inputs(seed: int = 0) -> dict:
    seeds = jax.random.split(jax.random.key(seed), 7)
    return {
        "query_vectors": draw_query_vectors(jax.random.fold_in(seeds[6], 71), 0),
        "key_vectors": draw_key_vectors(jax.random.fold_in(seeds[6], 71), 0),
        "value_vectors": normal_values(seeds[2], (GROUPS, GROUP_LEN, D), 1.0, 6.0, ((0, 4), (1, 128))),
        "levels": plant(jax.random.randint(seeds[3], (GROUPS,), 0, LEVELS), jax.random.fold_in(seeds[3], 1), 0, LEVELS - 1).astype(jnp.int32),
        "causal_order": draw_causal_order(jax.random.fold_in(seeds[6], 71), 0),
        "level_gates": jnp.clip(jax.random.uniform(seeds[5], (LEVELS, D), jnp.float32, 0.25, 2.0), 0.25, 2.0),
    }


def attend_head(query_head, key_head, value_head, visible):
    scores = jnp.dot(query_head, key_head.T, preferred_element_type=jnp.float32) * (HD ** -0.5)
    scores = jnp.where(visible[None, :], scores, -jnp.inf)
    top_score = jnp.max(scores, axis=-1, keepdims=True)
    weights = jnp.exp(scores - top_score)
    total = jnp.sum(weights, axis=-1, keepdims=True)
    mixed = jnp.dot(weights.astype(jnp.bfloat16), value_head, preferred_element_type=jnp.float32)
    return (mixed / total).astype(jnp.bfloat16)


def reference(query_vectors, key_vectors, value_vectors, levels, causal_order, level_gates):
    key_heads = key_vectors.reshape(GROUPS * GROUP_LEN, HEADS, HD).transpose(1, 0, 2)
    value_heads = value_vectors.reshape(GROUPS * GROUP_LEN, HEADS, HD).transpose(1, 0, 2)
    outputs = []
    for member in range(GROUPS):
        visible = jnp.repeat(causal_order <= causal_order[member], GROUP_LEN)
        query_heads = query_vectors[member].reshape(GROUP_LEN, HEADS, HD).transpose(1, 0, 2)
        attended = lax.map(lambda triple: attend_head(triple[0], triple[1], triple[2], visible), (query_heads, key_heads, value_heads))
        joined = attended.transpose(1, 0, 2).reshape(GROUP_LEN, HEADS * HD)
        gate_row = level_gates[levels[member]]
        outputs.append((joined.astype(jnp.float32) * gate_row[None, :]).astype(jnp.bfloat16))
    return jnp.stack(outputs)
```

```python
import jax
import jax.numpy as jnp
from jax import lax
from jax.experimental import pallas as pl
from jax.experimental.pallas import tpu as pltpu
from jax.sharding import PartitionSpec as P

HEADS = 32
HD = 128
GROUPS = 4
ROWS = 24
PAD = 32
SLOTS = 32
PART = 192
SUBSETS = 4
FOLD = HD**-0.5 * 1.4426950408889634
BF16, F32 = jnp.bfloat16, jnp.float32
MESH = pl.DeviceIdType.MESH
VMEM = pl.BlockSpec(memory_space=pltpu.VMEM)
SMEM = pl.BlockSpec(memory_space=pltpu.SMEM)


class Place:
    def __init__(self):
        seq = lax.axis_index("seq")
        self.x = lax.axis_index("group")
        self.core = seq % 2
        self.y = (seq // 2) % 8
        self.z = seq // 16
        self.pair, self.j = self.y // 2, self.y % 2

    def at(self, x, y, z, core):
        return {"group": x % 4, "seq": ((z % 8) * 8 + y % 8) * 2 + core}

    def target(self, dz, r):
        pair = (self.pair + r) % 4
        e = (self.y - 2 * pair + 7) % 8
        j = 1 - e // 4
        slot = j * e + (1 - j) * (7 - e)
        z = (self.z - dz) % 8
        return z * 4 + pair, 2 * pair + j, z, dz * 4 + slot

    def source(self, dz, slot):
        return (self.y + (2 * self.j - 1) * slot + 8) % 8, (self.z + dz) % 8


def remote(src, dst, send, recv, device):
    return pltpu.make_async_remote_copy(src, dst, send, recv, device_id=device, device_id_type=MESH)


def landed(ref, sem):
    pltpu.make_async_copy(ref, ref, sem).wait()


def head_columns(head):
    return pl.ds(pl.multiple_of(head * HD, HD), HD)


def side_by_side(two):
    return jnp.concatenate([two[0].astype(F32), two[1].astype(F32)], axis=0).astype(BF16)


def gather_kernel(
    q_ref, k_ref, v_ref, q_all, kv_all, q_stage, kv_stage, q_got, kv_got, send_sem, q_sem, kv_sem, near_sem, far_sem, core_sem, pair_sem
):
    me = Place()
    x, y, z, core = me.x, me.y, me.z, me.core
    right, left = me.at(x + 1, y, z, core), me.at(x + 3, y, z, core)
    other_core = me.at(x, y, z, 1 - core)
    partner = me.at(x, y + 1 - 2 * me.j, z, core)

    barrier = pltpu.get_barrier_semaphore()

    def greet(device):
        pl.semaphore_signal(barrier, inc=1, device_id=device, device_id_type=MESH)

    def greet_kv(i, carry):
        ys, zs = me.source(i // 4, i % 4)
        greet(me.at(x, ys, zs, core))
        return carry

    def greet_q(i, carry):
        dz = i // 4
        ys, zs = me.source(dz, i % 4)
        greet(me.at(x - dz + 8, ys, zs, core))
        return carry

    lax.fori_loop(1, SLOTS, greet_kv, 0)
    lax.fori_loop(4, 16, greet_q, 0)
    lax.fori_loop(20, SLOTS, greet_q, 0)
    for device in (right, left, other_core, partner):
        greet(device)

    def stage(h, carry):
        columns = head_columns(h)
        q_stage[h, :ROWS] = q_ref[0, :, columns]
        q_stage[h, ROWS:] = jnp.zeros((PAD - ROWS, HD), BF16)
        kv_stage[h] = side_by_side((k_ref[0, :, columns], v_ref[0, :, columns]))
        return carry

    lax.fori_loop(0, HEADS, stage, 0)
    own = z * 4 + me.pair
    q_got[0] = q_stage[own]
    kv_got[0] = kv_stage[own]
    pl.semaphore_wait(barrier, 31 + 24 + 4)

    def send_q(i, carry):
        dz = i // 4
        head, yd, zd, slot = me.target(dz, i % 4)
        remote(q_stage.at[head], q_got.at[slot], send_sem.at[0], q_sem, me.at(x + dz, yd, zd, core)).start()
        return carry

    def send_kv(i, carry):
        dz = i // 4
        head, yd, zd, slot = me.target(dz, i % 4)
        remote(kv_stage.at[head], kv_got.at[slot], send_sem.at[1], kv_sem.at[dz // 2], me.at(x, yd, zd, core)).start()
        return carry

    lax.fori_loop(1, SLOTS, send_kv, 0)
    lax.fori_loop(1, SLOTS, send_q, 0)

    def block(group, t, which):
        return kv_all.at[group, :, t, which]

    sent = []

    def push(src, dst, sem, recv, device):
        copy = remote(src, dst, sem, recv, device)
        copy.start()
        sent.append(copy)

    def own_part(t):
        first = 1 if t == 0 else 0
        landed(kv_got.at[pl.ds(t * 8 + first, 8 - first)], kv_sem.at[t])
        for i in range(4):
            two = kv_got[t * 8 + 2 * i], kv_got[t * 8 + 2 * i + 1]
            rows = pl.ds(i * 48, 48)
            kv_all[x, 0, t, core, rows] = side_by_side((two[0][:ROWS], two[1][:ROWS]))
            kv_all[x, 1, t, core, rows] = side_by_side((two[0][ROWS:], two[1][ROWS:]))
        mine = block(x, t, core)
        push(mine, mine, send_sem.at[2 + t], near_sem.at[0, t], right)
        push(mine, mine, send_sem.at[6 + t], near_sem.at[1, t], left)
        push(mine, mine, send_sem.at[10 + t], core_sem.at[0, t], other_core)

    def forward(t):
        from_left, from_right = (x + 3) % 4, (x + 1) % 4
        landed(block(from_left, t, core), near_sem.at[0, t])
        keys = kv_all.at[from_left, 0, t, core]
        push(keys, keys, send_sem.at[14 + t], far_sem.at[0, t], right)
        held = block(from_left, t, core)
        push(held, held, send_sem.at[18 + t], core_sem.at[1, t], other_core)
        landed(block(from_right, t, core), near_sem.at[1, t])
        values = kv_all.at[from_right, 1, t, core]
        push(values, values, send_sem.at[22 + t], far_sem.at[1, t], left)
        held = block(from_right, t, core)
        push(held, held, send_sem.at[26 + t], core_sem.at[2, t], other_core)

    def last(t):
        far = (x + 2) % 4
        landed(kv_all.at[far, 0, t, core], far_sem.at[0, t])
        landed(kv_all.at[far, 1, t, core], far_sem.at[1, t])
        held = block(far, t, core)
        push(held, held, send_sem.at[30 + t], core_sem.at[3, t], other_core)

    for step in range(SUBSETS + 2):
        if step < SUBSETS:
            own_part(step)
        if 0 <= step - 1 < SUBSETS:
            forward(step - 1)
        if 0 <= step - 2 < SUBSETS:
            last(step - 2)

    landed(q_got.at[pl.ds(1, SLOTS - 1)], q_sem)
    for dz in range(4):
        group = (x + 4 - dz) % 4
        for i in range(4):
            slot = dz * 4 + (i // 2) * 16 + (i % 2) * 2
            two = q_got[slot, :ROWS], q_got[slot + 1, :ROWS]
            q_all[me.j, group, pl.ds(i * 48, 48)] = side_by_side(two)
    push(q_all.at[me.j], q_all.at[me.j], send_sem.at[34], pair_sem, partner)

    for t in range(SUBSETS):
        for i, dx in enumerate((0, 3, 1, 2)):
            landed(block((x + dx) % 4, t, 1 - core), core_sem.at[i, t])
    landed(q_all.at[1 - me.j], pair_sem)
    landed(q_stage.at[pl.ds(1, SLOTS - 1)], send_sem.at[0])
    landed(kv_stage.at[pl.ds(1, SLOTS - 1)], send_sem.at[1])
    for copy in sent:
        copy.wait_send()


def gather(q, k, v):
    return pl.pallas_call(
        gather_kernel,
        out_shape=(
            jax.ShapeDtypeStruct((2, GROUPS, PART, HD), BF16),
            jax.ShapeDtypeStruct((GROUPS, 2, SUBSETS, 2, PART, HD), BF16),
        ),
        in_specs=[VMEM] * 3,
        out_specs=(VMEM, VMEM),
        scratch_shapes=[
            pltpu.VMEM((HEADS, PAD, HD), BF16),
            pltpu.VMEM((HEADS, 2 * ROWS, HD), BF16),
            pltpu.VMEM((SLOTS, PAD, HD), BF16),
            pltpu.VMEM((SLOTS, 2 * ROWS, HD), BF16),
            pltpu.SemaphoreType.DMA((35,)),
            pltpu.SemaphoreType.DMA,
            pltpu.SemaphoreType.DMA((SUBSETS,)),
            pltpu.SemaphoreType.DMA((2, SUBSETS)),
            pltpu.SemaphoreType.DMA((2, SUBSETS)),
            pltpu.SemaphoreType.DMA((4, SUBSETS)),
            pltpu.SemaphoreType.DMA,
        ],
        compiler_params=pltpu.CompilerParams(collective_id=0, has_side_effects=True, vmem_limit_bytes=48 * 2**20),
        name="gather",
    )(q, k, v)


def attend_kernel(order_ref, q_ref, kv_ref, o_ref, lse_ref, kk_ref, vv_ref):
    ranks = []
    for g in range(GROUPS):
        ranks.append(sum((order_ref[o] < order_ref[g]).astype(jnp.int32) for o in range(GROUPS)))
    at_rank = [sum(jnp.where(ranks[g] == r, g, 0) for g in range(GROUPS)) for r in range(GROUPS)]
    keys = kv_ref.shape[2]
    for r in range(GROUPS):
        k = kv_ref[at_rank[r], 0]
        kk_ref[r] = jnp.concatenate([k, k], axis=1)
        vv_ref[r] = jnp.concatenate([kv_ref[at_rank[r], 1], jnp.ones((keys, HD), BF16)], axis=1)
    for r in range(GROUPS):
        group = at_rank[r]
        for j in range(2):
            q = q_ref[j, group].astype(F32) * FOLD
            high = q.astype(BF16)
            q = jnp.concatenate([high, (q - high.astype(F32)).astype(BF16)], axis=1)
            top = total = None
            for other in range(r + 1):
                scores = lax.dot_general(q, kk_ref[other], (((1,), (1,)), ((), ())), preferred_element_type=F32)
                new_top = jnp.max(scores, axis=-1, keepdims=True)
                if other:
                    new_top = jnp.maximum(top, new_top)
                weights = jnp.exp2(scores - new_top).astype(BF16)
                mixed = jnp.dot(weights, vv_ref[other], preferred_element_type=F32)
                total = mixed if other == 0 else total * jnp.exp2(top - new_top) + mixed
                top = new_top
            row_sum = total[:, HD : HD + 1]
            o_ref[j, group] = total[:, :HD] / row_sum
            lse = top + jnp.log2(row_sum)
            for i in range(0, PART, 64):
                lse_ref[j, group, pl.ds(i // 64, 1)] = to_lanes(lse[i : i + 64])


def diagonal():
    return lax.broadcasted_iota(jnp.int32, (64, HD), 0) == lax.broadcasted_iota(jnp.int32, (64, HD), 1)


def to_lanes(column):
    return jnp.sum(jnp.where(diagonal(), column, 0.0), axis=0, keepdims=True)


def to_column(lanes):
    return jnp.sum(jnp.where(diagonal(), lanes, 0.0), axis=1, keepdims=True)


def attend(order, q, kv):
    kv = kv.reshape(GROUPS, 2, SUBSETS * 2 * PART, HD)
    keys = kv.shape[2]
    return pl.pallas_call(
        attend_kernel,
        out_shape=(
            jax.ShapeDtypeStruct((2, GROUPS, PART, HD), F32),
            jax.ShapeDtypeStruct((2, GROUPS, 8, HD), F32),
        ),
        in_specs=[SMEM, VMEM, VMEM],
        out_specs=(VMEM, VMEM),
        scratch_shapes=[
            pltpu.VMEM((GROUPS, keys, 2 * HD), BF16),
            pltpu.VMEM((GROUPS, keys, 2 * HD), BF16),
        ],
        compiler_params=pltpu.CompilerParams(vmem_limit_bytes=48 * 2**20),
        name="attend",
    )(order, q, kv)


def scatter_kernel(o_ref, lse_ref, out_ref, o_out, o_in, lse_out, lse_in, stage_ref, got, sems, home_sem):
    me = Place()
    x, y, z, core = me.x, me.y, me.z, me.core
    partner = me.at(x, y + 1 - 2 * me.j, z, core)
    barrier = pltpu.get_barrier_semaphore()

    def greet(i, carry):
        dz = i // 4
        _, yd, zd, _ = me.target(dz, i % 4)
        pl.semaphore_signal(barrier, inc=1, device_id=me.at(x + dz, yd, zd, core), device_id_type=MESH)
        return carry

    lax.fori_loop(1, SLOTS, greet, 0)
    pl.semaphore_signal(barrier, inc=1, device_id=partner, device_id_type=MESH)
    for g in range(GROUPS):
        o_out[g] = o_ref[1 - me.j, g].astype(BF16)
        lse_out[g] = lse_ref[1 - me.j, g]
    pl.semaphore_wait(barrier, SLOTS)
    give_o = remote(o_out, o_in, sems.at[0], sems.at[1], partner)
    give_lse = remote(lse_out, lse_in, sems.at[2], sems.at[3], partner)
    give_lse.start()
    give_o.start()
    give_lse.wait()
    give_o.wait()
    for dz in range(4):
        group = (x + 4 - dz) % 4
        for i in range(3):
            rows = pl.ds(i * 64, 64)
            difference = lse_in[group, pl.ds(i, 1)] - lse_ref[me.j, group, pl.ds(i, 1)]
            weight = to_column(1.0 / (1.0 + jnp.exp2(difference)))
            theirs = o_in[group, rows].astype(F32)
            o_ref_rows = o_ref[me.j, group, rows]
            merged = theirs + (o_ref_rows - theirs) * weight
            for part in range(8):
                run = i * 8 + part
                slot = dz * 4 + (run // 12) * 16 + (run // 3) % 4
                stage_ref[slot, pl.ds((run % 3) * 8, 8)] = merged[part * 8 : part * 8 + 8].astype(BF16)
        for i in range(8):
            stage_ref[dz * 4 + (i // 4) * 16 + i % 4, ROWS:] = jnp.zeros((PAD - ROWS, HD), BF16)
    own = z * 4 + me.pair
    got[own] = stage_ref[0]

    def send(i, carry):
        dz = i // 4
        ys, zs = me.source(dz, i % 4)
        remote(stage_ref.at[i], got.at[own], sems.at[4], home_sem, me.at(x - dz + 8, ys, zs, core)).start()
        return carry

    lax.fori_loop(1, SLOTS, send, 0)
    landed(got.at[pl.ds(1, SLOTS - 1)], home_sem)
    for h in range(HEADS):
        out_ref[:, h * HD : (h + 1) * HD] = got[h, :ROWS]
    landed(stage_ref.at[pl.ds(1, SLOTS - 1)], sems.at[4])


def scatter(o, lse):
    return pl.pallas_call(
        scatter_kernel,
        out_shape=jax.ShapeDtypeStruct((ROWS, HEADS * HD), BF16),
        in_specs=[VMEM, VMEM],
        out_specs=VMEM,
        scratch_shapes=[
            pltpu.VMEM((GROUPS, PART, HD), BF16),
            pltpu.VMEM((GROUPS, PART, HD), BF16),
            pltpu.VMEM((GROUPS, 8, HD), F32),
            pltpu.VMEM((GROUPS, 8, HD), F32),
            pltpu.VMEM((SLOTS, PAD, HD), BF16),
            pltpu.VMEM((HEADS, PAD, HD), BF16),
            pltpu.SemaphoreType.DMA((5,)),
            pltpu.SemaphoreType.DMA,
        ],
        compiler_params=pltpu.CompilerParams(collective_id=1, has_side_effects=True, vmem_limit_bytes=48 * 2**20),
        name="scatter",
    )(o, lse)


def shards(query_vectors, key_vectors, value_vectors, levels, causal_order, level_gates):
    q, kv = gather(query_vectors, key_vectors, value_vectors)
    joined = scatter(*attend(causal_order, q, kv))
    level = lax.dynamic_index_in_dim(levels, lax.axis_index("group"), keepdims=False)
    gate_row = lax.dynamic_index_in_dim(level_gates, level, keepdims=False)
    return (joined.astype(F32) * gate_row[None, :]).astype(BF16)[None]


def solution(mesh):
    placed = P("group", "seq", None)
    return jax.shard_map(
        shards, mesh=mesh, in_specs=(placed, placed, placed, P(), P(), P()), out_specs=placed, check_vma=False
    )
```

```python
import jax
import jax.numpy as jnp
from jax import lax
from jax.experimental import pallas as pl
from jax.experimental.pallas import tpu as pltpu
from jax.sharding import PartitionSpec as P

HEADS = 32
HD = 128
GROUPS = 4
ROWS = 24
PAD = 32
SLOTS = 32
PART = 192
SUBSETS = 4
FOLD = HD**-0.5 * 1.4426950408889634
BF16, F32 = jnp.bfloat16, jnp.float32
MESH = pl.DeviceIdType.MESH


def rem(a, n):
    return lax.rem(a, jnp.int32(n))


class Place:
    def __init__(self):
        seq = lax.axis_index("seq")
        self.x = lax.axis_index("group")
        self.core = rem(seq, 2)
        self.y = rem(seq // 2, 8)
        self.z = seq // 16
        self.pair, self.j = self.y // 2, rem(self.y, 2)
        self.xs = [self.x] + [rem(self.x + i, 4) for i in range(1, 4)]
        self.zs = [self.z] + [rem(self.z + i, 8) for i in range(1, 8)]
        self.holders = []
        for r in range(4):
            pair = rem(self.pair + r, 4)
            e = rem(self.y - 2 * pair + 15, 8)
            j = 1 - e // 4
            slot = j * e + (1 - j) * (7 - e)
            self.holders.append((pair, (2 * pair + j) * 2 + self.core, slot))
        self.senders = [rem(self.y + (2 * self.j - 1) * slot + 8, 8) * 2 + self.core for slot in range(4)]

    def at(self, x, y, z, core):
        return {"group": x, "seq": z * 16 + y * 2 + core}

    def target(self, i):
        dz, r = i // 4, i % 4
        pair, low, slot = self.holders[r]
        z = self.zs[-dz % 8]
        return z * 4 + pair, dz * 4 + slot, z * 16 + low, self.xs[dz % 4]

    def source(self, i):
        dz, slot = i // 4, i % 4
        return self.zs[dz] * 16 + self.senders[slot], self.xs[-dz % 4]


def remote(src, dst, send, recv, device):
    return pltpu.make_async_remote_copy(src, dst, send, recv, device_id=device, device_id_type=MESH)


def landed(ref, sem):
    pltpu.make_async_copy(ref, ref, sem).wait()


def side_by_side(two):
    return jnp.concatenate([two[0].astype(F32), two[1].astype(F32)], axis=0).astype(BF16)


def diagonal():
    return lax.broadcasted_iota(jnp.int32, (64, HD), 0) == lax.broadcasted_iota(jnp.int32, (64, HD), 1)


def to_lanes(rows):
    return jnp.sum(jnp.where(diagonal(), rows, 0.0), axis=0, keepdims=True)


def to_column(lanes):
    return jnp.sum(jnp.where(diagonal(), lanes, 0.0), axis=1, keepdims=True)


def kernel(
    levels_ref, order_ref, q_hbm, k_hbm, v_hbm, gates_hbm, out_ref,
    q_ref, k_ref, v_ref, gates_ref, q_stage, kv_stage, q_got, kv_got, q_all, kv_0, kv_1, kv_2, kv_3, qq_ref, top_ref, total_ref,
    o_out, o_in, lse_out, lse_in, merged_ref, home_stage, home_got,
    load_sem, send_sem, q_sem, kv_sem, near_sem, far_sem, core_sem, pair_sem, o_sem, lse_sem, home_sem,
):
    me = Place()
    x, y, z, core = me.x, me.y, me.z, me.core
    right, left = me.at(me.xs[1], y, z, core), me.at(me.xs[3], y, z, core)
    other_core = me.at(x, y, z, 1 - core)
    partner = me.at(x, y + 1 - 2 * me.j, z, core)
    own = z * 4 + me.pair
    kv_all = kv_0, kv_1, kv_2, kv_3

    loads = [
        pltpu.make_async_copy(src, dst, load_sem.at[i])
        for i, (src, dst) in enumerate(((q_hbm.at[0], q_ref), (k_hbm.at[0], k_ref), (v_hbm.at[0], v_ref), (gates_hbm, gates_ref)))
    ]
    for copy in loads:
        copy.start()

    barrier = pltpu.get_barrier_semaphore()

    def greet(device):
        pl.semaphore_signal(barrier, inc=1, device_id=device, device_id_type=MESH)

    for i in range(1, SLOTS):
        seq, xq = me.source(i)
        greet({"group": x, "seq": seq})
        if (i // 4) % 4:
            greet({"group": xq, "seq": seq})
        _, _, seq, xq = me.target(i)
        greet({"group": xq, "seq": seq})
    for device in (right, left, other_core, partner):
        greet(device)

    for copy in loads:
        copy.wait()

    def stage(h, carry):
        columns = pl.ds(pl.multiple_of(h * HD, HD), HD)
        q_stage[h, :ROWS] = q_ref[:, columns]
        q_stage[h, ROWS:] = jnp.zeros((PAD - ROWS, HD), BF16)
        kv_stage[h] = side_by_side((k_ref[:, columns], v_ref[:, columns]))
        return carry

    lax.fori_loop(0, HEADS, stage, 0, unroll=4)
    q_got[0] = q_stage[own]
    kv_got[0] = kv_stage[own]
    pl.semaphore_wait(barrier, 31 + 24 + 31 + 4)

    for i in range(1, SLOTS):
        head, slot, seq, xq = me.target(i)
        remote(q_stage.at[head], q_got.at[slot], send_sem.at[0], q_sem, {"group": xq, "seq": seq}).start()
    for i in range(1, SLOTS):
        head, slot, seq, _ = me.target(i)
        remote(kv_stage.at[head], kv_got.at[slot], send_sem.at[1], kv_sem.at[i // 8], {"group": x, "seq": seq}).start()

    sent = []

    def push(src, dst, recv, device):
        copy = remote(src, dst, send_sem.at[3 + len(sent)], recv, device)
        copy.start()
        sent.append(copy)

    def part_of(group, t, which):
        return kv_all[t].at[group, :, which]

    def own_part(t):
        first = 1 if t == 0 else 0
        landed(kv_got.at[pl.ds(t * 8 + first, 8 - first)], kv_sem.at[t])
        for i in range(4):
            two = kv_got[t * 8 + 2 * i], kv_got[t * 8 + 2 * i + 1]
            rows = pl.ds(i * 48, 48)
            kv_all[t][x, 0, core, rows] = side_by_side((two[0][:ROWS], two[1][:ROWS]))
            kv_all[t][x, 1, core, rows] = side_by_side((two[0][ROWS:], two[1][ROWS:]))
        mine = part_of(x, t, core)
        push(mine, mine, near_sem.at[0, t], right)
        push(mine, mine, near_sem.at[1, t], left)
        push(mine, mine, core_sem.at[0, t], other_core)

    def forward(t):
        from_left, from_right = me.xs[3], me.xs[1]
        landed(part_of(from_left, t, core), near_sem.at[0, t])
        keys = kv_all[t].at[from_left, 0, core]
        push(keys, keys, far_sem.at[0, t], right)
        held = part_of(from_left, t, core)
        push(held, held, core_sem.at[1, t], other_core)
        landed(part_of(from_right, t, core), near_sem.at[1, t])
        values = kv_all[t].at[from_right, 1, core]
        push(values, values, far_sem.at[1, t], left)
        held = part_of(from_right, t, core)
        push(held, held, core_sem.at[2, t], other_core)

    def far(t):
        opposite = me.xs[2]
        landed(kv_all[t].at[opposite, 0, core], far_sem.at[0, t])
        landed(kv_all[t].at[opposite, 1, core], far_sem.at[1, t])
        held = part_of(opposite, t, core)
        push(held, held, core_sem.at[3, t], other_core)

    def arrive(t):
        for i, dx in enumerate((0, 3, 1, 2)):
            landed(part_of(me.xs[dx], t, 1 - core), core_sem.at[i, t])

    def queries():
        landed(q_got.at[pl.ds(1, SLOTS - 1)], q_sem)
        for dz in range(4):
            group = me.xs[-dz % 4]
            for i in range(4):
                slot = dz * 4 + (i // 2) * 16 + (i % 2) * 2
                q_all[me.j, group, pl.ds(i * 48, 48)] = side_by_side((q_got[slot, :ROWS], q_got[slot + 1, :ROWS]))
            push(q_all.at[me.j, group], q_all.at[me.j, group], pair_sem.at[dz], partner)

    def before(o, g):
        return (order_ref[o] <= order_ref[g] if o < g else order_ref[o] < order_ref[g]).astype(jnp.int32)

    ranks = [sum(before(o, g) for o in range(GROUPS) if o != g) for g in range(GROUPS)]
    at_rank = [sum(jnp.where(ranks[g] == r, g, 0) for g in range(GROUPS)) for r in range(GROUPS)]

    def queries_of_pair():
        for dz in range(4):
            landed(q_all.at[1 - me.j, me.xs[-dz % 4]], pair_sem.at[dz])
        for r in range(GROUPS):
            for i, j in enumerate((1 - me.j, me.j)):
                qq_ref[pl.ds((2 * r + i) * PART, PART)] = q_all[j, at_rank[r]]

    count = 2 * PART

    def scores_of(t, other):
        keys = kv_all[t][at_rank[other], 0].reshape(count, HD)
        queries = qq_ref[pl.ds(other * count, (GROUPS - other) * count)]
        return lax.dot_general(queries, keys, (((1,), (1,)), ((), ())), preferred_element_type=F32) * FOLD

    def add(t, other, scores):
        rows = pl.ds(other * count, (GROUPS - other) * count)
        values = jnp.concatenate([kv_all[t][at_rank[other], 1].reshape(count, HD), jnp.ones((count, HD), BF16)], axis=1)
        top = jnp.max(scores, axis=-1, keepdims=True)
        if t or other:
            before = top_ref[rows]
            now = jnp.maximum(before, top)
            weights = jnp.exp2(scores - now[:, :1]).astype(BF16)
            mixed = jnp.dot(weights, values, preferred_element_type=F32)
            shrink = jnp.exp2(before - now)
            total_ref[rows, :HD] = total_ref[rows, :HD] * shrink + mixed[:, :HD]
            total_ref[rows, HD:] = total_ref[rows, HD:] * shrink + mixed[:, HD:]
            top_ref[rows] = now
        else:
            weights = jnp.exp2(scores - top).astype(BF16)
            total_ref[rows] = jnp.dot(weights, values, preferred_element_type=F32)
            top_ref[rows] = jnp.broadcast_to(top, (scores.shape[0], HD))

    def attend(t):
        scores = scores_of(t, 0)
        for other in range(GROUPS):
            following = scores_of(t, other + 1) if other + 1 < GROUPS else None
            add(t, other, scores)
            scores = following

    own_part(0)
    queries()
    own_part(1)
    forward(0)
    own_part(2)
    forward(1)
    far(0)
    queries_of_pair()
    own_part(3)
    forward(2)
    far(1)
    arrive(0)
    attend(0)
    forward(3)
    far(2)
    arrive(1)
    attend(1)
    far(3)
    arrive(2)
    attend(2)
    arrive(3)
    attend(3)

    for r in range(GROUPS):
        rows = pl.ds(2 * r * PART, PART)
        sums = total_ref[rows, HD:]
        o_out[r] = (total_ref[rows, :HD] / sums).astype(BF16)
        lse = top_ref[rows] + jnp.log2(sums)
        lse_out[r] = jnp.concatenate([to_lanes(lse[i : i + 64]) for i in range(0, PART, 64)] + [jnp.zeros((5, HD), F32)], axis=0)
        push(lse_out.at[r], lse_in.at[r], lse_sem.at[r], partner)
        push(o_out.at[r], o_in.at[r], o_sem.at[r], partner)
    for r in range(GROUPS):
        rows = pl.ds((2 * r + 1) * PART, PART)
        sums = total_ref[rows, HD:]
        mine = total_ref[rows, :HD] / sums
        lse = top_ref[rows] + jnp.log2(sums)
        landed(lse_in.at[r], lse_sem.at[r])
        landed(o_in.at[r], o_sem.at[r])
        for i in range(3):
            theirs = o_in[r, pl.ds(i * 64, 64)].astype(F32)
            weight = 1.0 / (1.0 + jnp.exp2(to_column(lse_in[r, pl.ds(i, 1)]) - lse[i * 64 : i * 64 + 64]))
            merged_ref[r, pl.ds(i * 64, 64)] = theirs + (mine[i * 64 : i * 64 + 64] - theirs) * weight

    for dz in range(4):
        group = me.xs[-dz % 4]
        rank = sum(jnp.where(group == g, ranks[g], 0) for g in range(GROUPS))
        merged = merged_ref[rank].astype(F32)
        for i in range(8):
            slot = dz * 4 + (i // 4) * 16 + i % 4
            home_stage[slot, :ROWS] = merged[i * ROWS : i * ROWS + ROWS].astype(BF16)
            home_stage[slot, ROWS:] = jnp.zeros((PAD - ROWS, HD), BF16)
            if slot == 0:
                home_got[own] = home_stage[0]
            else:
                seq, xq = me.source(slot)
                remote(home_stage.at[slot], home_got.at[own], send_sem.at[2], home_sem, {"group": xq, "seq": seq}).start()

    level = levels_ref[x]
    gate = gates_ref[pl.ds(level, 1)]
    landed(home_got.at[pl.ds(1, SLOTS - 1)], home_sem)
    for h in range(HEADS):
        columns = slice(h * HD, h * HD + HD)
        out_ref[0, :, columns] = (home_got[h, :ROWS].astype(F32) * gate[:, columns]).astype(BF16)
    landed(q_stage.at[pl.ds(1, SLOTS - 1)], send_sem.at[0])
    landed(kv_stage.at[pl.ds(1, SLOTS - 1)], send_sem.at[1])
    landed(home_stage.at[pl.ds(1, SLOTS - 1)], send_sem.at[2])
    for copy in sent:
        copy.wait_send()


def shards(query_vectors, key_vectors, value_vectors, levels, causal_order, level_gates):
    vmem, dma = pltpu.VMEM, pltpu.SemaphoreType.DMA
    smem, anywhere = pl.BlockSpec(memory_space=pltpu.SMEM), pl.BlockSpec(memory_space=pl.ANY)
    wide = HEADS * HD
    return pl.pallas_call(
        kernel,
        out_shape=jax.ShapeDtypeStruct((1, ROWS, wide), BF16),
        in_specs=[smem, smem, anywhere, anywhere, anywhere, anywhere],
        out_specs=pl.BlockSpec(memory_space=vmem),
        scratch_shapes=[
            *[vmem((ROWS, wide), BF16)] * 3,
            vmem(level_gates.shape, F32),
            *[vmem((HEADS, PAD, HD), BF16), vmem((HEADS, 2 * ROWS, HD), BF16)] * 2,
            vmem((2, GROUPS, PART, HD), BF16),
            *[vmem((GROUPS, 2, 2, PART, HD), BF16)] * SUBSETS,
            vmem((2 * GROUPS * PART, HD), BF16),
            vmem((2 * GROUPS * PART, HD), F32),
            vmem((2 * GROUPS * PART, 2 * HD), F32),
            *[vmem((GROUPS, PART, HD), BF16)] * 2,
            *[vmem((GROUPS, 8, HD), F32)] * 2,
            vmem((GROUPS, PART, HD), F32),
            *[vmem((HEADS, PAD, HD), BF16)] * 2,
            dma((4,)), dma((64,)), dma, dma((SUBSETS,)), dma((2, SUBSETS)), dma((2, SUBSETS)), dma((4, SUBSETS)),
            dma((GROUPS,)), dma((GROUPS,)), dma((GROUPS,)), dma,
        ],
        compiler_params=pltpu.CompilerParams(collective_id=0, has_side_effects=True, vmem_limit_bytes=56 * 2**20),
        name="attention",
    )(levels, causal_order, query_vectors, key_vectors, value_vectors, level_gates)


def solution(mesh):
    placed = P("group", "seq", None)
    return jax.shard_map(
        shards, mesh=mesh, in_specs=(placed, placed, placed, P(), P(), P()), out_specs=placed, check_vma=False
    )
```

```python
import jax
import jax.numpy as jnp
from jax import lax
from jax.experimental import pallas as pl
from jax.experimental.pallas import tpu as pltpu
from jax.sharding import PartitionSpec as P

HEADS = 32
HD = 128
GROUPS = 4
ROWS = 24
PAD = 32
SLOTS = 32
PART = 192
SUBSETS = 4
ORDER = (1, 7, 2, 6, 3, 5, 4, 0)
SELF = 4 * ORDER.index(0)
REMOTE = [i for i in range(SLOTS) if i != SELF]
FOLD = HD**-0.5 * 1.4426950408889634
BF16, F32 = jnp.bfloat16, jnp.float32
MESH = pl.DeviceIdType.MESH


def rem(a, n):
    return lax.rem(a, jnp.int32(n))


class Place:
    def __init__(self):
        seq = lax.axis_index("seq")
        self.x = lax.axis_index("group")
        self.core = rem(seq, 2)
        self.y = rem(seq // 2, 8)
        self.z = seq // 16
        self.pair, self.j = self.y // 2, rem(self.y, 2)
        self.xs = [self.x] + [rem(self.x + i, 4) for i in range(1, 4)]
        self.zs = [self.z] + [rem(self.z + i, 8) for i in range(1, 8)]
        self.holders = []
        for r in range(4):
            pair = rem(self.pair + r, 4)
            e = rem(self.y - 2 * pair + 15, 8)
            j = 1 - e // 4
            slot = j * e + (1 - j) * (7 - e)
            self.holders.append((pair, (2 * pair + j) * 2 + self.core, slot))
        self.senders = [rem(self.y + (2 * self.j - 1) * slot + 8, 8) * 2 + self.core for slot in range(4)]

    def at(self, x, y, z, core):
        return {"group": x, "seq": z * 16 + y * 2 + core}

    def target(self, i):
        dz, r = ORDER[i // 4], i % 4
        pair, low, slot = self.holders[r]
        z = self.zs[-dz % 8]
        return z * 4 + pair, i // 4 * 4 + slot, z * 16 + low, self.xs[dz % 4]

    def source(self, i):
        dz, slot = ORDER[i // 4], i % 4
        return self.zs[dz] * 16 + self.senders[slot], self.xs[-dz % 4]


def remote(src, dst, send, recv, device):
    return pltpu.make_async_remote_copy(src, dst, send, recv, device_id=device, device_id_type=MESH)


def landed(ref, sem):
    pltpu.make_async_copy(ref, ref, sem).wait()


def side_by_side(two):
    return jnp.concatenate([two[0].astype(F32), two[1].astype(F32)], axis=0).astype(BF16)


def diagonal():
    return lax.broadcasted_iota(jnp.int32, (64, HD), 0) == lax.broadcasted_iota(jnp.int32, (64, HD), 1)


def to_lanes(rows):
    return jnp.sum(jnp.where(diagonal(), rows, 0.0), axis=0, keepdims=True)


def to_column(lanes):
    return jnp.sum(jnp.where(diagonal(), lanes, 0.0), axis=1, keepdims=True)


def kernel(
    levels_ref, order_ref, q_hbm, k_hbm, v_hbm, gates_hbm, out_ref, gate_ref,
    q_ref, k_ref, v_ref, gates_ref, q_stage, kv_stage, q_got, kv_got, q_all, kv_0, kv_1, kv_2, kv_3, qq_ref, top_ref, total_ref,
    o_out, o_in, lse_out, lse_in, merged_ref, home_stage, home_got,
    load_sem, send_sem, q_sem, kv_sem, near_sem, far_sem, core_sem, pair_sem, o_sem, lse_sem, home_sem,
):
    me = Place()
    x, y, z, core = me.x, me.y, me.z, me.core
    right, left = me.at(me.xs[1], y, z, core), me.at(me.xs[3], y, z, core)
    other_core = me.at(x, y, z, 1 - core)
    partner = me.at(x, y + 1 - 2 * me.j, z, core)
    own = z * 4 + me.pair
    kv_all = kv_0, kv_1, kv_2, kv_3

    loads = [
        pltpu.make_async_copy(src, dst, load_sem.at[i])
        for i, (src, dst) in enumerate(((q_hbm.at[0], q_ref), (k_hbm.at[0], k_ref), (v_hbm.at[0], v_ref), (gates_hbm, gates_ref)))
    ]
    for copy in loads:
        copy.start()

    barrier = pltpu.get_barrier_semaphore()

    def greet(device):
        pl.semaphore_signal(barrier, inc=1, device_id=device, device_id_type=MESH)

    for i in reversed(REMOTE):
        seq, xq = me.source(i)
        greet({"group": x, "seq": seq})
        if ORDER[i // 4] % 4:
            greet({"group": xq, "seq": seq})
    for device in (right, left, other_core, partner):
        greet(device)

    for copy in loads:
        copy.wait()

    def stage(h, carry):
        columns = pl.ds(pl.multiple_of(h * HD, HD), HD)
        q_stage[h, :ROWS] = q_ref[:, columns]
        q_stage[h, ROWS:] = jnp.zeros((PAD - ROWS, HD), BF16)
        kv_stage[h] = side_by_side((k_ref[:, columns], v_ref[:, columns]))
        return carry

    lax.fori_loop(0, HEADS, stage, 0, unroll=4)
    q_got[SELF] = q_stage[own]
    kv_got[SELF] = kv_stage[own]
    pl.semaphore_wait(barrier, 31 + 24 + 4)

    def send_q():
        for i in REMOTE:
            head, slot, seq, xq = me.target(i)
            remote(q_stage.at[head], q_got.at[slot], send_sem.at[0], q_sem, {"group": xq, "seq": seq}).start()

    def send_kv(t):
        for i in REMOTE:
            if i // 8 == t:
                head, slot, seq, _ = me.target(i)
                remote(kv_stage.at[head], kv_got.at[slot], send_sem.at[1], kv_sem.at[t], {"group": x, "seq": seq}).start()

    send_q()
    send_kv(0)
    send_kv(1)
    send_kv(2)
    send_kv(3)

    sent = []

    def push(src, dst, recv, device, pieces=1):
        sem, rows = send_sem.at[3 + len(sent)], src.shape[0] // pieces
        for i in range(pieces):
            piece = pl.ds(i * rows, rows)
            remote(src.at[piece], dst.at[piece], sem, recv, device).start()
        sent.append(remote(src, dst, sem, recv, device))

    def part_of(group, t, which):
        return kv_all[t].at[group, which]

    def own_part(t):
        landed(kv_got.at[pl.ds(t * 8, 7 if t == SELF // 8 else 8)], kv_sem.at[t])
        for i in range(4):
            two = kv_got[t * 8 + 2 * i], kv_got[t * 8 + 2 * i + 1]
            rows = pl.ds(i * 48, 48)
            kv_all[t][x, core, 0, rows] = side_by_side((two[0][:ROWS], two[1][:ROWS]))
            kv_all[t][x, core, 1, rows] = side_by_side((two[0][ROWS:], two[1][ROWS:]))
        mine = part_of(x, t, core)
        push(mine, mine, core_sem.at[0, t], other_core)
        push(mine, mine, near_sem.at[0, t], right)
        push(mine, mine, near_sem.at[1, t], left)

    def forward(t):
        from_left, from_right = me.xs[3], me.xs[1]
        landed(part_of(from_left, t, core), near_sem.at[0, t])
        held = part_of(from_left, t, core)
        push(held, held, core_sem.at[1, t], other_core)
        keys = kv_all[t].at[from_left, core, 0]
        push(keys, keys, far_sem.at[0, t], right)
        landed(part_of(from_right, t, core), near_sem.at[1, t])
        held = part_of(from_right, t, core)
        push(held, held, core_sem.at[2, t], other_core)
        values = kv_all[t].at[from_right, core, 1]
        push(values, values, far_sem.at[1, t], left)

    def far(t):
        opposite = me.xs[2]
        landed(kv_all[t].at[opposite, core, 0], far_sem.at[0, t])
        landed(kv_all[t].at[opposite, core, 1], far_sem.at[1, t])
        held = part_of(opposite, t, core)
        push(held, held, core_sem.at[3, t], other_core)

    def arrive(t):
        for i, dx in enumerate((0, 3, 1, 2)):
            landed(part_of(me.xs[dx], t, 1 - core), core_sem.at[i, t])

    def queries():
        landed(q_got.at[pl.ds(1, SLOTS - 1)], q_sem)
        for dz in range(4):
            group = me.xs[-dz % 4]
            for i in range(4):
                slot = 4 * ORDER.index(dz + i // 2 * 4) + i % 2 * 2
                q_all[me.j, group, pl.ds(i * 48, 48)] = side_by_side((q_got[slot, :ROWS], q_got[slot + 1, :ROWS]))
            push(q_all.at[me.j, group], q_all.at[me.j, group], pair_sem.at[dz], partner, 4)

    def before(o, g):
        return (order_ref[o] <= order_ref[g] if o < g else order_ref[o] < order_ref[g]).astype(jnp.int32)

    ranks = [sum(before(o, g) for o in range(GROUPS) if o != g) for g in range(GROUPS)]
    at_rank = [sum(jnp.where(ranks[g] == r, g, 0) for g in range(GROUPS)) for r in range(GROUPS)]

    def queries_of_pair():
        for dz in range(4):
            landed(q_all.at[1 - me.j, me.xs[-dz % 4]], pair_sem.at[dz])
        for r in range(GROUPS):
            for i, j in enumerate((1 - me.j, me.j)):
                qq_ref[pl.ds((2 * r + i) * PART, PART)] = q_all[j, at_rank[r]]

    count = 2 * PART

    def scores_of(t, other):
        keys = kv_all[t][at_rank[other], :, 0].reshape(count, HD)
        queries = qq_ref[pl.ds(other * count, (GROUPS - other) * count)]
        return lax.dot_general(queries, keys, (((1,), (1,)), ((), ())), preferred_element_type=F32) * FOLD

    def add(t, other, scores):
        rows = pl.ds(other * count, (GROUPS - other) * count)
        values = jnp.concatenate([kv_all[t][at_rank[other], :, 1].reshape(count, HD), jnp.ones((count, HD), BF16)], axis=1)
        top = jnp.max(scores, axis=-1, keepdims=True)
        if t or other:
            before = top_ref[rows]
            now = jnp.maximum(before, top)
            weights = jnp.exp2(scores - now[:, :1]).astype(BF16)
            mixed = jnp.dot(weights, values, preferred_element_type=F32)
            shrink = jnp.exp2(before - now)
            total_ref[rows, :HD] = total_ref[rows, :HD] * shrink + mixed[:, :HD]
            total_ref[rows, HD:] = total_ref[rows, HD:] * shrink + mixed[:, HD:]
            top_ref[rows] = now
        else:
            weights = jnp.exp2(scores - top).astype(BF16)
            total_ref[rows] = jnp.dot(weights, values, preferred_element_type=F32)
            top_ref[rows] = jnp.broadcast_to(top, (scores.shape[0], HD))

    def finish(r):
        rows = pl.ds(2 * r * PART, PART)
        sums = total_ref[rows, HD:]
        o_out[r] = (total_ref[rows, :HD] / sums).astype(BF16)
        lse = top_ref[rows] + jnp.log2(sums)
        lse_out[r] = jnp.concatenate([to_lanes(lse[i : i + 64]) for i in range(0, PART, 64)] + [jnp.zeros((5, HD), F32)], axis=0)
        push(lse_out.at[r], lse_in.at[r], lse_sem.at[r], partner)
        push(o_out.at[r], o_in.at[r], o_sem.at[r], partner, 4)

    def meanwhile(t):
        if t == 0:
            forward(3)
            far(2)
        if t == 1:
            far(3)
        arrive(t + 1)

    def attend():
        blocks = [(t, other) for t in range(SUBSETS) for other in range(GROUPS)]
        scores = scores_of(0, 0)
        for i, (t, other) in enumerate(blocks):
            if other == GROUPS - 1 and t < SUBSETS - 1:
                meanwhile(t)
            following = scores_of(*blocks[i + 1]) if i + 1 < len(blocks) else None
            add(t, other, scores)
            if t == SUBSETS - 1:
                finish(other)
            scores = following

    own_part(0)
    queries()
    own_part(1)
    forward(0)
    own_part(2)
    forward(1)
    far(0)
    queries_of_pair()
    own_part(3)
    forward(2)
    far(1)
    arrive(0)
    attend()

    for r in range(GROUPS):
        rows = pl.ds((2 * r + 1) * PART, PART)
        sums = total_ref[rows, HD:]
        mine = total_ref[rows, :HD] / sums
        lse = top_ref[rows] + jnp.log2(sums)
        landed(lse_in.at[r], lse_sem.at[r])
        landed(o_in.at[r], o_sem.at[r])
        for i in range(3):
            theirs = o_in[r, pl.ds(i * 64, 64)].astype(F32)
            weight = 1.0 / (1.0 + jnp.exp2(to_column(lse_in[r, pl.ds(i, 1)]) - lse[i * 64 : i * 64 + 64]))
            merged_ref[r, pl.ds(i * 64, 64)] = theirs + (mine[i * 64 : i * 64 + 64] - theirs) * weight

    for dz in range(4):
        group = me.xs[-dz % 4]
        rank = sum(jnp.where(group == g, ranks[g], 0) for g in range(GROUPS))
        merged = merged_ref[rank].astype(F32)
        for i in range(8):
            slot = 4 * ORDER.index(dz + i // 4 * 4) + i % 4
            home_stage[slot, :ROWS] = merged[i * ROWS : i * ROWS + ROWS].astype(BF16)
            home_stage[slot, ROWS:] = jnp.zeros((PAD - ROWS, HD), BF16)
            if slot == SELF:
                home_got[own] = home_stage[SELF]
            else:
                seq, xq = me.source(slot)
                remote(home_stage.at[slot], home_got.at[own], send_sem.at[2], home_sem, {"group": xq, "seq": seq}).start()

    gate_ref[...] = gates_ref[pl.ds(levels_ref[x], 1)]
    landed(home_got.at[pl.ds(1, SLOTS - 1)], home_sem)
    for h in range(HEADS):
        columns = slice(h * HD, h * HD + HD)
        out_ref[:, columns] = home_got[h, :ROWS]
    landed(q_stage.at[pl.ds(1, SLOTS - 1)], send_sem.at[0])
    landed(kv_stage.at[pl.ds(1, SLOTS - 1)], send_sem.at[1])
    landed(home_stage.at[pl.ds(1, SLOTS - 1)], send_sem.at[2])
    for copy in sent:
        copy.wait_send()


def shards(query_vectors, key_vectors, value_vectors, levels, causal_order, level_gates):
    vmem, dma = pltpu.VMEM, pltpu.SemaphoreType.DMA
    smem, anywhere = pl.BlockSpec(memory_space=pltpu.SMEM), pl.BlockSpec(memory_space=pl.ANY)
    wide = HEADS * HD
    joined, gate = pl.pallas_call(
        kernel,
        out_shape=(jax.ShapeDtypeStruct((ROWS, wide), BF16), jax.ShapeDtypeStruct((1, wide), F32)),
        in_specs=[smem, smem, anywhere, anywhere, anywhere, anywhere],
        out_specs=(pl.BlockSpec(memory_space=vmem), pl.BlockSpec(memory_space=vmem)),
        scratch_shapes=[
            *[vmem((ROWS, wide), BF16)] * 3,
            vmem(level_gates.shape, F32),
            *[vmem((HEADS, PAD, HD), BF16), vmem((HEADS, 2 * ROWS, HD), BF16)] * 2,
            vmem((2, GROUPS, PART, HD), BF16),
            *[vmem((GROUPS, 2, 2, PART, HD), BF16)] * SUBSETS,
            vmem((2 * GROUPS * PART, HD), BF16),
            vmem((2 * GROUPS * PART, HD), F32),
            vmem((2 * GROUPS * PART, 2 * HD), F32),
            *[vmem((GROUPS, PART, HD), BF16)] * 2,
            *[vmem((GROUPS, 8, HD), F32)] * 2,
            vmem((GROUPS, PART, HD), F32),
            *[vmem((HEADS, PAD, HD), BF16)] * 2,
            dma((4,)), dma((64,)), dma, dma((SUBSETS,)), dma((2, SUBSETS)), dma((2, SUBSETS)), dma((4, SUBSETS)),
            dma((GROUPS,)), dma((GROUPS,)), dma((GROUPS,)), dma,
        ],
        compiler_params=pltpu.CompilerParams(collective_id=0, has_side_effects=True, vmem_limit_bytes=56 * 2**20),
        name="attention",
    )(levels, causal_order, query_vectors, key_vectors, value_vectors, level_gates)
    return (joined.astype(F32) * gate).astype(BF16)[None]


def solution(mesh):
    placed = P("group", "seq", None)
    return jax.shard_map(
        shards, mesh=mesh, in_specs=(placed, placed, placed, P(), P(), P()), out_specs=placed, check_vma=False
    )
```

```python
import jax
import jax.numpy as jnp
from jax import lax
from jax.experimental import pallas as pl
from jax.experimental.pallas import tpu as pltpu
from jax.sharding import PartitionSpec as P

HEADS = 32
HD = 128
GROUPS = 4
ROWS = 24
PAD = 32
SLOTS = 32
PART = 192
SIZES = (8, 8, 8, 8)
SUBSETS = len(SIZES)
STARTS = [sum(SIZES[:t]) for t in range(SUBSETS)]
ORDER = (0, 1, 7, 2, 6, 3, 5, 4)
SELF = 4 * ORDER.index(0)
REMOTE = [i for i in range(SLOTS) if i != SELF]
FOLD = HD**-0.5 * 1.4426950408889634
BF16, F32 = jnp.bfloat16, jnp.float32
MESH = pl.DeviceIdType.MESH


def rem(a, n):
    return lax.rem(a, jnp.int32(n))


class Place:
    def __init__(self):
        seq = lax.axis_index("seq")
        self.x = lax.axis_index("group")
        self.core = rem(seq, 2)
        self.y = rem(seq // 2, 8)
        self.z = seq // 16
        self.pair, self.j = self.y // 2, rem(self.y, 2)
        self.xs = [self.x] + [rem(self.x + i, 4) for i in range(1, 4)]
        self.zs = [self.z] + [rem(self.z + i, 8) for i in range(1, 8)]
        self.holders = []
        for r in range(4):
            pair = rem(self.pair + r, 4)
            e = rem(self.y - 2 * pair + 15, 8)
            j = 1 - e // 4
            slot = j * e + (1 - j) * (7 - e)
            self.holders.append((pair, (2 * pair + j) * 2 + self.core, slot))
        self.senders = [rem(self.y + (2 * self.j - 1) * slot + 8, 8) * 2 + self.core for slot in range(4)]

    def at(self, x, y, z, core):
        return {"group": x, "seq": z * 16 + y * 2 + core}

    def target(self, i):
        dz, r = ORDER[i // 4], i % 4
        pair, low, slot = self.holders[r]
        z = self.zs[-dz % 8]
        return z * 4 + pair, i // 4 * 4 + slot, z * 16 + low, self.xs[dz % 4]

    def source(self, i):
        dz, slot = ORDER[i // 4], i % 4
        return self.zs[dz] * 16 + self.senders[slot], self.xs[-dz % 4]


def remote(src, dst, send, recv, device):
    return pltpu.make_async_remote_copy(src, dst, send, recv, device_id=device, device_id_type=MESH)


def landed(ref, sem):
    pltpu.make_async_copy(ref, ref, sem).wait()


def side_by_side(two):
    return jnp.concatenate([two[0].astype(F32), two[1].astype(F32)], axis=0).astype(BF16)


def diagonal():
    return lax.broadcasted_iota(jnp.int32, (64, HD), 0) == lax.broadcasted_iota(jnp.int32, (64, HD), 1)


def to_lanes(rows):
    return jnp.sum(jnp.where(diagonal(), rows, 0.0), axis=0, keepdims=True)


def to_column(lanes):
    return jnp.sum(jnp.where(diagonal(), lanes, 0.0), axis=1, keepdims=True)


def kernel(
    levels_ref, order_ref, q_hbm, k_hbm, v_hbm, gates_hbm, out_ref, gate_ref,
    q_ref, k_ref, v_ref, gates_ref, q_stage, kv_stage, q_got, kv_got, q_all, kv_0, kv_1, kv_2, kv_3, qq_ref, top_ref, total_ref,
    o_out, o_in, lse_out, lse_in, merged_ref, home_stage, home_got,
    load_sem, send_sem, q_sem, kv_sem, near_sem, far_sem, core_sem, pair_sem, o_sem, lse_sem, home_sem,
):
    me = Place()
    x, y, z, core = me.x, me.y, me.z, me.core
    right, left = me.at(me.xs[1], y, z, core), me.at(me.xs[3], y, z, core)
    other_core = me.at(x, y, z, 1 - core)
    partner = me.at(x, y + 1 - 2 * me.j, z, core)
    own = z * 4 + me.pair
    kv_all = kv_0, kv_1, kv_2, kv_3

    loads = [
        pltpu.make_async_copy(src, dst, load_sem.at[i])
        for i, (src, dst) in enumerate(((q_hbm.at[0], q_ref), (k_hbm.at[0], k_ref), (v_hbm.at[0], v_ref), (gates_hbm, gates_ref)))
    ]
    for copy in loads:
        copy.start()

    barrier = pltpu.get_barrier_semaphore()

    def greet(device):
        pl.semaphore_signal(barrier, inc=1, device_id=device, device_id_type=MESH)

    for i in reversed(REMOTE):
        seq, xq = me.source(i)
        greet({"group": x, "seq": seq})
        if ORDER[i // 4] % 4:
            greet({"group": xq, "seq": seq})
    for device in (right, left, other_core, partner):
        greet(device)

    for copy in loads:
        copy.wait()

    def stage(h, carry):
        columns = pl.ds(pl.multiple_of(h * HD, HD), HD)
        q_stage[h, :ROWS] = q_ref[:, columns]
        q_stage[h, ROWS:] = jnp.zeros((PAD - ROWS, HD), BF16)
        kv_stage[h] = side_by_side((k_ref[:, columns], v_ref[:, columns]))
        return carry

    lax.fori_loop(0, HEADS, stage, 0, unroll=4)
    q_got[SELF] = q_stage[own]
    kv_got[SELF] = kv_stage[own]
    pl.semaphore_wait(barrier, 31 + 24 + 4)

    def send_q():
        for i in REMOTE:
            head, slot, seq, xq = me.target(i)
            remote(q_stage.at[head], q_got.at[slot], send_sem.at[0], q_sem, {"group": xq, "seq": seq}).start()

    def send_kv(t):
        for i in REMOTE:
            if STARTS[t] <= i < STARTS[t] + SIZES[t]:
                head, slot, seq, _ = me.target(i)
                remote(kv_stage.at[head], kv_got.at[slot], send_sem.at[1], kv_sem.at[t], {"group": x, "seq": seq}).start()

    send_q()
    send_kv(0)
    send_kv(1)
    send_kv(2)
    send_kv(3)

    sent = []

    def push(src, dst, recv, device, pieces=1):
        sem, rows = send_sem.at[3 + len(sent)], src.shape[0] // pieces
        for i in range(pieces):
            piece = pl.ds(i * rows, rows)
            remote(src.at[piece], dst.at[piece], sem, recv, device).start()
        sent.append(remote(src, dst, sem, recv, device))

    def part_of(group, t, which):
        return kv_all[t].at[group, which]

    def own_part(t):
        first, size = STARTS[t], SIZES[t]
        landed(kv_got.at[pl.ds(first, size - int(first <= SELF < first + size))], kv_sem.at[t])
        for i in range(size // 2):
            two = kv_got[first + 2 * i], kv_got[first + 2 * i + 1]
            rows = pl.ds(i * 48, 48)
            kv_all[t][x, core, 0, rows] = side_by_side((two[0][:ROWS], two[1][:ROWS]))
            kv_all[t][x, core, 1, rows] = side_by_side((two[0][ROWS:], two[1][ROWS:]))
        mine = part_of(x, t, core)
        push(mine, mine, core_sem.at[0, t], other_core)
        push(mine, mine, near_sem.at[0, t], right)
        push(mine, mine, near_sem.at[1, t], left)

    def forward(t):
        from_left, from_right = me.xs[3], me.xs[1]
        landed(part_of(from_left, t, core), near_sem.at[0, t])
        held = part_of(from_left, t, core)
        push(held, held, core_sem.at[1, t], other_core)
        keys = kv_all[t].at[from_left, core, 0]
        push(keys, keys, far_sem.at[0, t], right)
        landed(part_of(from_right, t, core), near_sem.at[1, t])
        held = part_of(from_right, t, core)
        push(held, held, core_sem.at[2, t], other_core)
        values = kv_all[t].at[from_right, core, 1]
        push(values, values, far_sem.at[1, t], left)

    def far(t):
        opposite = me.xs[2]
        landed(kv_all[t].at[opposite, core, 0], far_sem.at[0, t])
        landed(kv_all[t].at[opposite, core, 1], far_sem.at[1, t])
        held = part_of(opposite, t, core)
        push(held, held, core_sem.at[3, t], other_core)

    def arrive(t):
        for i, dx in enumerate((0, 3, 1, 2)):
            landed(part_of(me.xs[dx], t, 1 - core), core_sem.at[i, t])

    def queries():
        landed(q_got.at[pl.ds(1, SLOTS - 1)], q_sem)
        for dz in range(4):
            group = me.xs[-dz % 4]
            for i in range(4):
                slot = 4 * ORDER.index(dz + i // 2 * 4) + i % 2 * 2
                q_all[me.j, group, pl.ds(i * 48, 48)] = side_by_side((q_got[slot, :ROWS], q_got[slot + 1, :ROWS]))
            push(q_all.at[me.j, group], q_all.at[me.j, group], pair_sem.at[dz], partner, 4)

    def before(o, g):
        return (order_ref[o] <= order_ref[g] if o < g else order_ref[o] < order_ref[g]).astype(jnp.int32)

    ranks = [sum(before(o, g) for o in range(GROUPS) if o != g) for g in range(GROUPS)]
    at_rank = [sum(jnp.where(ranks[g] == r, g, 0) for g in range(GROUPS)) for r in range(GROUPS)]

    def queries_of_pair():
        for dz in range(4):
            landed(q_all.at[1 - me.j, me.xs[-dz % 4]], pair_sem.at[dz])
        for r in range(GROUPS):
            for i, j in enumerate((1 - me.j, me.j)):
                qq_ref[pl.ds((2 * r + i) * PART, PART)] = q_all[j, at_rank[r]]

    count = 2 * PART

    def scores_of(t, other):
        keys = kv_all[t][at_rank[other], :, 0].reshape(2 * SIZES[t] * ROWS, HD)
        queries = qq_ref[pl.ds(other * count, (GROUPS - other) * count)]
        return lax.dot_general(queries, keys, (((1,), (1,)), ((), ())), preferred_element_type=F32) * FOLD

    def add(t, other, scores):
        rows = pl.ds(other * count, (GROUPS - other) * count)
        values = kv_all[t][at_rank[other], :, 1].reshape(2 * SIZES[t] * ROWS, HD)
        values = jnp.concatenate([values, jnp.ones(values.shape, BF16)], axis=1)
        top = jnp.max(scores, axis=-1, keepdims=True)
        if t or other:
            before = top_ref[rows]
            now = jnp.maximum(before, top)
            weights = jnp.exp2(scores - now[:, :1]).astype(BF16)
            mixed = jnp.dot(weights, values, preferred_element_type=F32)
            shrink = jnp.exp2(before - now)
            total_ref[rows, :HD] = total_ref[rows, :HD] * shrink + mixed[:, :HD]
            total_ref[rows, HD:] = total_ref[rows, HD:] * shrink + mixed[:, HD:]
            top_ref[rows] = now
        else:
            weights = jnp.exp2(scores - top).astype(BF16)
            total_ref[rows] = jnp.dot(weights, values, preferred_element_type=F32)
            top_ref[rows] = jnp.broadcast_to(top, (scores.shape[0], HD))

    def finish(r):
        rows = pl.ds(2 * r * PART, PART)
        sums = total_ref[rows, HD:]
        o_out[r] = (total_ref[rows, :HD] / sums).astype(BF16)
        lse = top_ref[rows] + jnp.log2(sums)
        lse_out[r] = jnp.concatenate([to_lanes(lse[i : i + 64]) for i in range(0, PART, 64)] + [jnp.zeros((5, HD), F32)], axis=0)
        push(lse_out.at[r], lse_in.at[r], lse_sem.at[r], partner)
        push(o_out.at[r], o_in.at[r], o_sem.at[r], partner, 4)

    MEANWHILE = {
        (0, 3): ((forward, 3), (far, 2), (arrive, 1)),
        (1, 3): ((far, 3), (arrive, 2)),
        (2, 3): ((arrive, 3),),
    }

    def attend():
        blocks = [(t, other) for t in range(SUBSETS) for other in range(GROUPS)]
        scores = scores_of(0, 0)
        for i, (t, other) in enumerate(blocks):
            for step, subset in MEANWHILE.get((t, other), ()):
                step(subset)
            following = scores_of(*blocks[i + 1]) if i + 1 < len(blocks) else None
            add(t, other, scores)
            if t == SUBSETS - 1:
                finish(other)
            scores = following

    own_part(0)
    queries()
    own_part(1)
    forward(0)
    own_part(2)
    forward(1)
    far(0)
    queries_of_pair()
    own_part(3)
    forward(2)
    far(1)
    arrive(0)
    attend()

    for r in range(GROUPS):
        rows = pl.ds((2 * r + 1) * PART, PART)
        sums = total_ref[rows, HD:]
        mine = total_ref[rows, :HD] / sums
        lse = top_ref[rows] + jnp.log2(sums)
        landed(lse_in.at[r], lse_sem.at[r])
        landed(o_in.at[r], o_sem.at[r])
        for i in range(3):
            theirs = o_in[r, pl.ds(i * 64, 64)].astype(F32)
            weight = 1.0 / (1.0 + jnp.exp2(to_column(lse_in[r, pl.ds(i, 1)]) - lse[i * 64 : i * 64 + 64]))
            merged_ref[r, pl.ds(i * 64, 64)] = theirs + (mine[i * 64 : i * 64 + 64] - theirs) * weight

    for dz in range(4):
        group = me.xs[-dz % 4]
        rank = sum(jnp.where(group == g, ranks[g], 0) for g in range(GROUPS))
        merged = merged_ref[rank].astype(F32)
        for i in range(8):
            slot = 4 * ORDER.index(dz + i // 4 * 4) + i % 4
            home_stage[slot, :ROWS] = merged[i * ROWS : i * ROWS + ROWS].astype(BF16)
            home_stage[slot, ROWS:] = jnp.zeros((PAD - ROWS, HD), BF16)
            if slot == SELF:
                home_got[own] = home_stage[SELF]
            else:
                seq, xq = me.source(slot)
                remote(home_stage.at[slot], home_got.at[own], send_sem.at[2], home_sem, {"group": xq, "seq": seq}).start()

    gate_ref[...] = gates_ref[pl.ds(levels_ref[x], 1)]
    landed(home_got.at[pl.ds(1, SLOTS - 1)], home_sem)
    for h in range(HEADS):
        columns = slice(h * HD, h * HD + HD)
        out_ref[:, columns] = home_got[h, :ROWS]
    landed(q_stage.at[pl.ds(1, SLOTS - 1)], send_sem.at[0])
    landed(kv_stage.at[pl.ds(1, SLOTS - 1)], send_sem.at[1])
    landed(home_stage.at[pl.ds(1, SLOTS - 1)], send_sem.at[2])
    for copy in sent:
        copy.wait_send()


def shards(query_vectors, key_vectors, value_vectors, levels, causal_order, level_gates):
    vmem, dma = pltpu.VMEM, pltpu.SemaphoreType.DMA
    smem, anywhere = pl.BlockSpec(memory_space=pltpu.SMEM), pl.BlockSpec(memory_space=pl.ANY)
    wide = HEADS * HD
    joined, gate = pl.pallas_call(
        kernel,
        out_shape=(jax.ShapeDtypeStruct((ROWS, wide), BF16), jax.ShapeDtypeStruct((1, wide), F32)),
        in_specs=[smem, smem, anywhere, anywhere, anywhere, anywhere],
        out_specs=(pl.BlockSpec(memory_space=vmem), pl.BlockSpec(memory_space=vmem)),
        scratch_shapes=[
            *[vmem((ROWS, wide), BF16)] * 3,
            vmem(level_gates.shape, F32),
            *[vmem((HEADS, PAD, HD), BF16), vmem((HEADS, 2 * ROWS, HD), BF16)] * 2,
            vmem((2, GROUPS, PART, HD), BF16),
            *[vmem((GROUPS, 2, 2, size * ROWS, HD), BF16) for size in SIZES],
            vmem((2 * GROUPS * PART, HD), BF16),
            vmem((2 * GROUPS * PART, HD), F32),
            vmem((2 * GROUPS * PART, 2 * HD), F32),
            *[vmem((GROUPS, PART, HD), BF16)] * 2,
            *[vmem((GROUPS, 8, HD), F32)] * 2,
            vmem((GROUPS, PART, HD), F32),
            *[vmem((HEADS, PAD, HD), BF16)] * 2,
            dma((4,)), dma((64,)), dma, dma((SUBSETS,)), dma((2, SUBSETS)), dma((2, SUBSETS)), dma((4, SUBSETS)),
            dma((GROUPS,)), dma((GROUPS,)), dma((GROUPS,)), dma,
        ],
        compiler_params=pltpu.CompilerParams(collective_id=0, has_side_effects=True, vmem_limit_bytes=56 * 2**20),
        name="attention",
    )(levels, causal_order, query_vectors, key_vectors, value_vectors, level_gates)
    return (joined.astype(F32) * gate).astype(BF16)[None]


def solution(mesh):
    placed = P("group", "seq", None)
    return jax.shard_map(
        shards, mesh=mesh, in_specs=(placed, placed, placed, P(), P(), P()), out_specs=placed, check_vma=False
    )
```
